32 devices in a mesh: groups: 2 (over y), tm: 4 (over x, core), space: 4 (over z).
Axes of the slice: x: 2, y: 2, z: 4, core: 2. Of those that a mesh axis runs over, the one named last changes fastest.
Arguments:
- initial_state: float32 [8, 32, 8, 128], P(None, ('groups', 'space')), parts along dimension 1, may hold values from -3 to 3
- first_guess: float32 [32, 8, 32, 8, 128], P('tm', None, ('groups', 'space')), parts along dimension 2, may hold values from -3 to 3
- diffusivity: float32 [8, 32, 8, 128], P(None, ('groups', 'space')), parts along dimension 1, may hold values from 0.02 to 0.2
- growth_rates: float32 [8], replicated, may hold values from -1 to 1
- coupling: float32 [8, 8], replicated, may hold values from -2 to 2
Outputs:
- iterate: float32 [32, 8, 32, 8, 128], P('tm', None, ('groups', 'space')), parts along dimension 2
The draws below stay inside these ranges and needn't reach their ends.
There are 2 independent parts, one for each index of `groups`. The reference program is written for one: setup_inputs(seed, part) draws one part's arguments, and reference() takes and returns one part's arrays. A program takes and returns all parts, laid end to end along the dimension named above; an argument that names none is the same for every part. Nothing has to cross between parts.
All inputs are finite; a program needn't handle non-finite values.
Results may differ from the reference program's by a relative error of at most 0.0001.
Values sent between devices are 32-bit elements; how exact they have to be, the bound alone decides.
A program may use at most 64 MiB of HBM per device.

```python
import math
import jax
import jax.numpy as jnp
from jax import lax

SPECIES = 8
NODES = 8
SWEEPS = 2
CY = 8
CZ = 128
NX = 16
STEPS = 32
N_TM = 4


def shard_levels(own_key, extent, pieces, least, high):
    gain = 1.0
    for axis_at, shards_of in pieces:
        draws = jax.random.uniform(jax.random.fold_in(jax.random.fold_in(own_key, 6), axis_at), (shards_of,), jnp.float32, least / len(pieces), high / len(pieces))
        gain = gain * jnp.repeat(jnp.exp(draws), extent[axis_at] // shards_of).reshape((-1,) + (1,) * (len(extent) - 1 - axis_at))
    return gain


def noise(own_key, shape, spread, reach, cuts=(), kind=jnp.bfloat16):
    gain = shard_levels(own_key, shape, cuts, -0.22, 0.18) if cuts else 1.0
    drawn = jax.random.normal(own_key, shape, jnp.float32) * spread * gain
    return jnp.minimum(jnp.maximum(drawn, -reach), reach).astype(kind)


def setup_inputs(seed: int = 0, part: int = 0) -> dict:
    streams_of = jax.random.split(jax.random.key(seed), 6)
    part_splits = jax.random.split(jax.random.fold_in(streams_of[5], part), 6)
    initial_state = noise(part_splits[0], (SPECIES, NX, CY, CZ), 0.7, 3.0, ((1, 4),), jnp.float32)
    first_guess = noise(part_splits[1], (STEPS, SPECIES, NX, CY, CZ), 0.7, 3.0, ((0, 4), (2, 4)), jnp.float32)
    diffusivity = jnp.clip(jnp.exp(math.log(0.2) - 2.3025851 * jax.random.uniform(part_splits[2], (SPECIES, NX, CY, CZ), jnp.float32) ** shard_levels(part_splits[2], (SPECIES, NX, CY, CZ), ((1, 4),), -0.2, 0.2)), 0.02, 0.2)
    growth_rates = jnp.clip(jax.random.uniform(streams_of[3], (SPECIES,), jnp.float32, -1.0, 1.0), -1.0, 1.0)
    coupling = noise(streams_of[4], (SPECIES, SPECIES), SPECIES ** -0.5, 2.0, (), jnp.float32)
    return dict(initial_state=initial_state, first_guess=first_guess, diffusivity=diffusivity, growth_rates=growth_rates, coupling=coupling)


slab_span = 0.025


def evaluate(coeffs, point):
    result = 0.0
    for entry in reversed(coeffs):
        result = result * point + entry
    return result


def quadrature(node_count):
    node_pos = [(index + 0.5) / node_count for index in range(node_count)]
    within_rows = [[0.0] * node_count for row_no in range(node_count)]
    whole_row = [0.0] * node_count
    for column in range(node_count):
        coeffs = [1.0]
        scale_value = 1.0
        for other_node in range(node_count):
            if other_node != column:
                shifted = [0.0] + coeffs
                for degree in range(len(coeffs)):
                    shifted[degree] = shifted[degree] - node_pos[other_node] * coeffs[degree]
                coeffs = shifted
                scale_value = scale_value * (node_pos[column] - node_pos[other_node])
        antider = [0.0] + [coeffs[degree] / (degree + 1) / scale_value for degree in range(len(coeffs))]
        for row_no in range(node_count):
            within_rows[row_no][column] = evaluate(antider, node_pos[row_no]) * slab_span
        whole_row[column] = evaluate(antider, 1.0) * slab_span
    return within_rows, whole_row


def fourth(field, axis_no):
    return (16.0 * (jnp.roll(field, 1, axis_no) + jnp.roll(field, -1, axis_no)) - (jnp.roll(field, 2, axis_no) + jnp.roll(field, -2, axis_no)) - 30.0 * field) / 12.0


def tendency(padded, center, diffusivity, growth_rates, coupling):
    along_x = (16.0 * (padded[:, :, 3:-1] + padded[:, :, 1:-3]) - (padded[:, :, 4:] + padded[:, :, :-4]) - 30.0 * center) / 12.0
    laplace = along_x + fourth(center, 3) + fourth(center, 4)
    mixing = jnp.einsum("sr,nrxyz->nsxyz", coupling, center, precision=lax.Precision.HIGHEST)
    return diffusivity[None] * laplace + growth_rates[None, :, None, None, None] * center - center * center * center / 3.0 + mixing


def reference(initial_state, first_guess, diffusivity, growth_rates, coupling):
    within_rows, whole_row = quadrature(NODES)
    within_table = jnp.asarray(within_rows, jnp.float32)
    whole_table = jnp.asarray(whole_row, jnp.float32)
    iterate = first_guess.reshape(N_TM, NODES, SPECIES, NX, CY, CZ)
    for sweep_no in range(SWEEPS):
        def one_slab(nodes_block):
            padded = jnp.pad(nodes_block, ((0, 0), (0, 0), (2, 2), (0, 0), (0, 0)))
            forcing = tendency(padded, nodes_block, diffusivity, growth_rates, coupling)
            local_part = jnp.einsum("mj,jsxyz->msxyz", within_table, forcing, precision=lax.Precision.HIGHEST)
            slab_total = jnp.einsum("j,jsxyz->sxyz", whole_table, forcing, precision=lax.Precision.HIGHEST)
            return local_part, slab_total

        local_part, totals = lax.map(one_slab, iterate)
        running = jnp.cumsum(totals, axis=0)
        preceding = jnp.concatenate([jnp.zeros_like(totals[:1]), running[:-1]], axis=0)
        iterate = initial_state[None, None] + preceding[:, None] + local_part
    return iterate.reshape(STEPS, SPECIES, NX, CY, CZ)
```

```python
import functools

import jax
import jax.numpy as jnp
from jax import lax
from jax.experimental import pallas as pl
from jax.experimental.pallas import tpu as pltpu
from jax.sharding import PartitionSpec as P

MESH = pl.DeviceIdType.MESH
slab_span = 0.025


def evaluate(coeffs, point):
    result = 0.0
    for entry in reversed(coeffs):
        result = result * point + entry
    return result


def quadrature(node_count):
    node_pos = [(index + 0.5) / node_count for index in range(node_count)]
    within_rows = [[0.0] * node_count for row_no in range(node_count)]
    whole_row = [0.0] * node_count
    for column in range(node_count):
        coeffs = [1.0]
        scale_value = 1.0
        for other_node in range(node_count):
            if other_node != column:
                shifted = [0.0] + coeffs
                for degree in range(len(coeffs)):
                    shifted[degree] = shifted[degree] - node_pos[other_node] * coeffs[degree]
                coeffs = shifted
                scale_value = scale_value * (node_pos[column] - node_pos[other_node])
        antider = [0.0] + [
            coeffs[degree] / (degree + 1) / scale_value for degree in range(len(coeffs))
        ]
        for row_no in range(node_count):
            within_rows[row_no][column] = evaluate(antider, node_pos[row_no]) * slab_span
        whole_row[column] = evaluate(antider, 1.0) * slab_span
    return (within_rows, whole_row)


def kernel(
    n_tm, n_z, within, whole,
    guess, init, diff, coupling, growth, out,
    u, base, u1, hal, d12, tsend1, trecv1, tsend2, trecv2,
    load_sem, out_sem, hs1, hr1, hs2, hr2, ts1, tr1, ts2, tr2,
):
    nodes, species, planes = u.shape[:3]
    tm = lax.axis_index("tm")
    z = lax.axis_index("space")
    groups = ((1, 2), (0, planes - 1))

    can_send = (z < n_z - 1, z > 0)
    has_recv = (z > 0, z < n_z - 1)

    def target(side):
        return {"space": z + 1} if side == 0 else {"space": z - 1}

    def edge(side, dist):
        return planes - 1 - dist if side == 0 else dist

    def halo1(side, dist):
        return pltpu.make_async_remote_copy(
            src_ref=guess.at[:, :, edge(side, dist)],
            dst_ref=hal.at[0, side, dist],
            send_sem=hs1.at[side, dist], recv_sem=hr1.at[side, dist],
            device_id=target(side), device_id_type=MESH,
        )

    def halo2(side, dist, s):
        return pltpu.make_async_remote_copy(
            src_ref=u1.at[:, s, edge(side, dist)],
            dst_ref=hal.at[1, side, dist, :, s],
            send_sem=hs2.at[side, dist, s], recv_sem=hr2.at[side, dist, s],
            device_id=target(side), device_id_type=MESH,
        )

    def total1(source, peer, g):
        return pltpu.make_async_remote_copy(
            src_ref=tsend1.at[g], dst_ref=trecv1.at[source, g],
            send_sem=ts1.at[peer, g], recv_sem=tr1.at[source, g],
            device_id={"tm": peer}, device_id_type=MESH,
        )

    def total2(source, peer, s):
        return pltpu.make_async_remote_copy(
            src_ref=tsend2.at[s], dst_ref=trecv2.at[source, s],
            send_sem=ts2.at[peer, s], recv_sem=tr2.at[source, s],
            device_id={"tm": peer}, device_id_type=MESH,
        )

    def loop(count, body, first=0):
        def step(i, carry):
            body(i)
            return carry
        lax.fori_loop(first, count, step, 0)

    load = pltpu.make_async_copy(guess, u, load_sem)
    load.start()

    barrier = pltpu.get_barrier_semaphore()
    for side in (0, 1):
        @pl.when(can_send[side])
        def _():
            pl.semaphore_signal(barrier, inc=1, device_id=target(side), device_id_type=MESH)
    for peer in range(n_tm):
        @pl.when(peer != tm)
        def _():
            pl.semaphore_signal(barrier, inc=1, device_id={"tm": peer}, device_id_type=MESH)
    neighbours = (z > 0).astype(jnp.int32) + (z < n_z - 1).astype(jnp.int32)
    pl.semaphore_wait(barrier, neighbours + n_tm - 1)

    for dist in (0, 1):
        for side in (0, 1):
            @pl.when(can_send[side])
            def _():
                halo1(side, dist).start()

    for side in (0, 1):
        @pl.when(jnp.logical_not(has_recv[side]))
        def _():
            def clear(s):
                for k in (0, 1):
                    for dist in (0, 1):
                        hal[k, side, dist, :, s] = jnp.zeros(
                            (nodes,) + hal.shape[5:], jnp.float32)
            loop(species, clear)

    d12[...] = diff[...] * (1.0 / 12.0)
    load.wait()

    def near_part(ref, s, p):
        c = ref[:, s, p]
        acc = growth[s] * c - c * c * c * (1.0 / 3.0)
        for r in range(species):
            acc = acc + coupling[s, r] * ref[:, r, p]
        near = pltpu.roll(c, 1, 1) + pltpu.roll(c, c.shape[1] - 1, 1)
        near = near + (pltpu.roll(c, 1, 2) + pltpu.roll(c, c.shape[2] - 1, 2))
        far = pltpu.roll(c, 2, 1) + pltpu.roll(c, c.shape[1] - 2, 1)
        far = far + (pltpu.roll(c, 2, 2) + pltpu.roll(c, c.shape[2] - 2, 2))
        for q in (p - 1, p + 1):
            if 0 <= q < planes:
                near = near + ref[:, s, q]
        for q in (p - 2, p + 2):
            if 0 <= q < planes:
                far = far + ref[:, s, q]
        base[:, s, p] = acc + d12[s, p][None] * (16.0 * near - far - 90.0 * c)

    def with_halo(k, s, p):
        if p == 0:
            add = 16.0 * hal[k, 0, 0, :, s] - hal[k, 0, 1, :, s]
        elif p == 1:
            add = -hal[k, 0, 0, :, s]
        elif p == planes - 1:
            add = 16.0 * hal[k, 1, 0, :, s] - hal[k, 1, 1, :, s]
        else:
            add = -hal[k, 1, 0, :, s]
        return base[:, s, p] + d12[s, p][None] * add

    def integrate(f, s, p):
        for m in range(nodes):
            row = within[m][0] * f[0]
            for j in range(1, nodes):
                row = row + within[m][j] * f[j]
            base[m, s, p] = row
        total = whole[0] * f[0]
        for j in range(1, nodes):
            total = total + whole[j] * f[j]
        return total

    def all_near(ref):
        def body(s):
            for p in range(planes):
                near_part(ref, s, p)
        loop(species, body)

    all_near(u)
    for g in (0, 1):
        for side in (0, 1):
            @pl.when(has_recv[side])
            def _():
                halo1(side, g).wait_recv()

        def finish(s):
            for i, p in enumerate(groups[g]):
                tsend1[g, s, i] = integrate(with_halo(0, s, p), s, p)
        loop(species, finish)
        loop(n_tm, lambda peer: total1(tm, peer, g).start(), tm + 1)
        loop(tm, lambda source: total1(source, tm, g).wait_recv())

        def advance(s):
            for i, p in enumerate(groups[g]):
                first = lax.fori_loop(
                    0, tm, lambda q, acc: acc + trecv1[q, g, s, i],
                    jnp.zeros(init.shape[2:], jnp.float32))
                u1[:, s, p] = base[:, s, p] + (init[s, p] + first)[None]
            for side in (0, 1):
                @pl.when(can_send[side])
                def _():
                    halo2(side, 1 - g, s).start()
        loop(species, advance)

    all_near(u1)
    for side in (0, 1):
        @pl.when(has_recv[side])
        def _():
            loop(species, lambda s: halo2(side, 1, s).wait_recv())

    def finish2(s):
        for side in (0, 1):
            @pl.when(has_recv[side])
            def _():
                halo2(side, 0, s).wait_recv()
        for p in range(planes):
            tsend2[s, p] = integrate(with_halo(1, s, p), s, p)
        loop(n_tm, lambda peer: total2(tm, peer, s).start(), tm + 1)
    loop(species, finish2)

    def store(s):
        return pltpu.make_async_copy(u.at[:, s], out.at[:, s], out_sem.at[s])

    def last(s):
        def gather(q, acc):
            total2(q, tm, s).wait_recv()
            return acc + trecv2[q, s]
        first = lax.fori_loop(0, tm, gather, init[s])
        u[:, s] = base[:, s] + first[None]
        store(s).start()
    loop(species, last)

    for side in (0, 1):
        @pl.when(can_send[side])
        def _():
            for dist in (0, 1):
                halo1(side, dist).wait_send()
                loop(species, lambda s: halo2(side, dist, s).wait_send())

    def sent(peer):
        for g in (0, 1):
            total1(tm, peer, g).wait_send()
        loop(species, lambda s: total2(tm, peer, s).wait_send())
    loop(n_tm, sent, tm + 1)
    loop(species, lambda s: store(s).wait())


def on_device(n_tm, n_z, initial_state, first_guess, diffusivity, growth_rates, coupling):
    nodes, species, planes, cy, cz = first_guess.shape
    within, whole = quadrature(nodes)
    vmem = pl.BlockSpec(memory_space=pltpu.VMEM)
    smem = pl.BlockSpec(memory_space=pltpu.SMEM)
    anywhere = pl.BlockSpec(memory_space=pl.ANY)
    f32 = jnp.float32
    block = pltpu.VMEM(first_guess.shape, f32)
    dma = pltpu.SemaphoreType.DMA
    return pl.pallas_call(
        functools.partial(kernel, n_tm, n_z, within, whole),
        out_shape=jax.ShapeDtypeStruct(first_guess.shape, f32),
        in_specs=[anywhere, vmem, vmem, smem, smem],
        out_specs=anywhere,
        scratch_shapes=[
            block, block, block,
            pltpu.VMEM((2, 2, 2, nodes, species, cy, cz), f32),
            pltpu.VMEM((species, planes, cy, cz), f32),
            pltpu.VMEM((2, species, 2, cy, cz), f32),
            pltpu.VMEM((n_tm, 2, species, 2, cy, cz), f32),
            pltpu.VMEM((species, planes, cy, cz), f32),
            pltpu.VMEM((n_tm, species, planes, cy, cz), f32),
            dma, dma((species,)),
            dma((2, 2)), dma((2, 2)),
            dma((2, 2, species)), dma((2, 2, species)),
            dma((n_tm, 2)), dma((n_tm, 2)),
            dma((n_tm, species)), dma((n_tm, species)),
        ],
        compiler_params=pltpu.CompilerParams(
            collective_id=0, has_side_effects=True, vmem_limit_bytes=32 * 1024 * 1024
        ),
        cost_estimate=pl.CostEstimate(
            flops=2 * 60 * first_guess.size, bytes_accessed=9 * first_guess.size,
            transcendentals=0),
    )(first_guess, initial_state, diffusivity, coupling, growth_rates)


def solution(mesh):
    in_specs = (
        P(None, ("groups", "space"), None, None),
        P("tm", None, ("groups", "space"), None, None),
        P(None, ("groups", "space"), None, None),
        P(),
        P(),
    )
    out_specs = P("tm", None, ("groups", "space"), None, None)
    return jax.shard_map(
        functools.partial(on_device, mesh.shape["tm"], mesh.shape["space"]),
        mesh=mesh, in_specs=in_specs, out_specs=out_specs, check_vma=False,
    )
```

```python
import functools

import jax
import jax.numpy as jnp
from jax import lax
from jax.experimental import pallas as pl
from jax.experimental.pallas import tpu as pltpu
from jax.sharding import PartitionSpec as P

MESH = pl.DeviceIdType.MESH
slab_span = 0.025


def evaluate(coeffs, point):
    result = 0.0
    for entry in reversed(coeffs):
        result = result * point + entry
    return result


def quadrature(node_count):
    node_pos = [(index + 0.5) / node_count for index in range(node_count)]
    within_rows = [[0.0] * node_count for row_no in range(node_count)]
    whole_row = [0.0] * node_count
    for column in range(node_count):
        coeffs = [1.0]
        scale_value = 1.0
        for other_node in range(node_count):
            if other_node != column:
                shifted = [0.0] + coeffs
                for degree in range(len(coeffs)):
                    shifted[degree] = shifted[degree] - node_pos[other_node] * coeffs[degree]
                coeffs = shifted
                scale_value = scale_value * (node_pos[column] - node_pos[other_node])
        antider = [0.0] + [
            coeffs[degree] / (degree + 1) / scale_value for degree in range(len(coeffs))
        ]
        for row_no in range(node_count):
            within_rows[row_no][column] = evaluate(antider, node_pos[row_no]) * slab_span
        whole_row[column] = evaluate(antider, 1.0) * slab_span
    return (within_rows, whole_row)


def kernel(
    n_tm, n_z, within, whole,
    guess, init_in, diff_in, coupling_in, growth_in, out,
    init, diff, coupling, growth, small_sem,
    u, base, u1, hal, d12, tsend1, trecv1, tsend2, trecv2,
    load_sem, out_sem, hs1, hr1, hs2, hr2, ts1, tr1, ts2, tr2,
):
    nodes, species, planes = u.shape[:3]
    tm = lax.axis_index("tm")
    z = lax.axis_index("space")
    groups = ((1, 2), (0, planes - 1))

    can_send = (z < n_z - 1, z > 0)
    has_recv = (z > 0, z < n_z - 1)

    def target(side):
        return {"space": z + 1} if side == 0 else {"space": z - 1}

    def edge(side, dist):
        return planes - 1 - dist if side == 0 else dist

    def halo1(side, dist):
        return pltpu.make_async_remote_copy(
            src_ref=guess.at[:, :, edge(side, dist)],
            dst_ref=hal.at[0, side, dist],
            send_sem=hs1.at[side, dist], recv_sem=hr1.at[side, dist],
            device_id=target(side), device_id_type=MESH,
        )

    def halo2(side, dist, s):
        return pltpu.make_async_remote_copy(
            src_ref=u1.at[:, s, edge(side, dist)],
            dst_ref=hal.at[1, side, dist, :, s],
            send_sem=hs2.at[side, dist, s], recv_sem=hr2.at[side, dist, s],
            device_id=target(side), device_id_type=MESH,
        )

    def total1(source, peer, g):
        return pltpu.make_async_remote_copy(
            src_ref=tsend1.at[g], dst_ref=trecv1.at[source, g],
            send_sem=ts1.at[peer, g], recv_sem=tr1.at[source, g],
            device_id={"tm": peer}, device_id_type=MESH,
        )

    def total2(source, peer, s):
        return pltpu.make_async_remote_copy(
            src_ref=tsend2.at[s], dst_ref=trecv2.at[source, s],
            send_sem=ts2.at[peer, s], recv_sem=tr2.at[source, s],
            device_id={"tm": peer}, device_id_type=MESH,
        )

    def loop(count, body, first=0):
        def step(i, carry):
            body(i)
            return carry
        lax.fori_loop(first, count, step, 0)

    load = pltpu.make_async_copy(guess, u, load_sem)
    load.start()
    small = [
        pltpu.make_async_copy(source, target_ref, small_sem.at[i])
        for i, (source, target_ref) in enumerate(
            ((init_in, init), (diff_in, diff), (coupling_in, coupling), (growth_in, growth)))
    ]
    for copy in small:
        copy.start()

    barrier = pltpu.get_barrier_semaphore()
    for side in (0, 1):
        @pl.when(can_send[side])
        def _():
            pl.semaphore_signal(barrier, inc=1, device_id=target(side), device_id_type=MESH)
    for peer in range(n_tm):
        @pl.when(peer != tm)
        def _():
            pl.semaphore_signal(barrier, inc=1, device_id={"tm": peer}, device_id_type=MESH)
    neighbours = (z > 0).astype(jnp.int32) + (z < n_z - 1).astype(jnp.int32)
    pl.semaphore_wait(barrier, neighbours + n_tm - 1)

    for side in (0, 1):
        @pl.when(can_send[side])
        def _():
            halo1(side, 0).start()

    for side in (0, 1):
        @pl.when(jnp.logical_not(has_recv[side]))
        def _():
            def clear(s):
                for k in (0, 1):
                    for dist in (0, 1):
                        hal[k, side, dist, :, s] = jnp.zeros(
                            (nodes,) + hal.shape[5:], jnp.float32)
            loop(species, clear)

    for copy in small:
        copy.wait()
    d12[...] = diff[...] * (1.0 / 12.0)
    load.wait()

    def near_part(ref, s, p):
        c = ref[:, s, p]
        acc = growth[s] * c - c * c * c * (1.0 / 3.0)
        for r in range(species):
            acc = acc + coupling[s, r] * ref[:, r, p]
        near = pltpu.roll(c, 1, 1) + pltpu.roll(c, c.shape[1] - 1, 1)
        near = near + (pltpu.roll(c, 1, 2) + pltpu.roll(c, c.shape[2] - 1, 2))
        far = pltpu.roll(c, 2, 1) + pltpu.roll(c, c.shape[1] - 2, 1)
        far = far + (pltpu.roll(c, 2, 2) + pltpu.roll(c, c.shape[2] - 2, 2))
        for q in (p - 1, p + 1):
            if 0 <= q < planes:
                near = near + ref[:, s, q]
        for q in (p - 2, p + 2):
            if 0 <= q < planes:
                far = far + ref[:, s, q]
        base[:, s, p] = acc + d12[s, p][None] * (16.0 * near - far - 90.0 * c)

    def with_halo(k, s, p):
        if p == 0:
            add = 16.0 * hal[k, 0, 0, :, s] - hal[k, 0, 1, :, s]
        elif p == 1:
            add = -hal[k, 0, 0, :, s]
        elif p == planes - 1:
            add = 16.0 * hal[k, 1, 0, :, s] - hal[k, 1, 1, :, s]
        else:
            add = -hal[k, 1, 0, :, s]
        return base[:, s, p] + d12[s, p][None] * add

    def integrate(f, s, p):
        for m in range(nodes):
            row = within[m][0] * f[0]
            for j in range(1, nodes):
                row = row + within[m][j] * f[j]
            base[m, s, p] = row
        total = whole[0] * f[0]
        for j in range(1, nodes):
            total = total + whole[j] * f[j]
        return total

    def all_near(ref):
        def body(s):
            for p in range(planes):
                near_part(ref, s, p)
        loop(species, body)

    all_near(u)
    for side in (0, 1):
        @pl.when(can_send[side])
        def _():
            halo1(side, 0).wait_send()
            halo1(side, 1).start()
    for g in (0, 1):
        for side in (0, 1):
            @pl.when(has_recv[side])
            def _():
                halo1(side, g).wait_recv()

        def finish(s):
            for i, p in enumerate(groups[g]):
                tsend1[g, s, i] = integrate(with_halo(0, s, p), s, p)
        loop(species, finish)
        loop(n_tm, lambda peer: total1(tm, peer, g).start(), tm + 1)
        loop(tm, lambda source: total1(source, tm, g).wait_recv())

        def advance(s):
            for i, p in enumerate(groups[g]):
                first = lax.fori_loop(
                    0, tm, lambda q, acc: acc + trecv1[q, g, s, i],
                    jnp.zeros(init.shape[2:], jnp.float32))
                u1[:, s, p] = base[:, s, p] + (init[s, p] + first)[None]
            for side in (0, 1):
                @pl.when(can_send[side])
                def _():
                    halo2(side, 1 - g, s).start()
        loop(species, advance)

    all_near(u1)
    for side in (0, 1):
        @pl.when(has_recv[side])
        def _():
            loop(species, lambda s: halo2(side, 1, s).wait_recv())

    def finish2(s):
        for side in (0, 1):
            @pl.when(has_recv[side])
            def _():
                halo2(side, 0, s).wait_recv()
        for p in range(planes):
            tsend2[s, p] = integrate(with_halo(1, s, p), s, p)
        loop(n_tm, lambda peer: total2(tm, peer, s).start(), tm + 1)
    loop(species, finish2)

    def store(s):
        return pltpu.make_async_copy(u.at[:, s], out.at[:, s], out_sem.at[s])

    def last(s):
        def gather(q, acc):
            total2(q, tm, s).wait_recv()
            return acc + trecv2[q, s]
        first = lax.fori_loop(0, tm, gather, init[s])
        u[:, s] = base[:, s] + first[None]
        store(s).start()
    loop(species, last)

    for side in (0, 1):
        @pl.when(can_send[side])
        def _():
            halo1(side, 1).wait_send()
            for dist in (0, 1):
                loop(species, lambda s: halo2(side, dist, s).wait_send())

    def sent(peer):
        for g in (0, 1):
            total1(tm, peer, g).wait_send()
        loop(species, lambda s: total2(tm, peer, s).wait_send())
    loop(n_tm, sent, tm + 1)
    loop(species, lambda s: store(s).wait())


def on_device(n_tm, n_z, initial_state, first_guess, diffusivity, growth_rates, coupling):
    nodes, species, planes, cy, cz = first_guess.shape
    within, whole = quadrature(nodes)
    hbm = pl.BlockSpec(memory_space=pltpu.HBM)
    f32 = jnp.float32
    block = pltpu.VMEM(first_guess.shape, f32)
    dma = pltpu.SemaphoreType.DMA
    return pl.pallas_call(
        functools.partial(kernel, n_tm, n_z, within, whole),
        out_shape=jax.ShapeDtypeStruct(first_guess.shape, f32),
        in_specs=[hbm] * 5,
        out_specs=hbm,
        scratch_shapes=[
            pltpu.VMEM((species, planes, cy, cz), f32),
            pltpu.VMEM((species, planes, cy, cz), f32),
            pltpu.SMEM(coupling.shape, f32),
            pltpu.SMEM(growth_rates.shape, f32),
            dma((4,)),
            block, block, block,
            pltpu.VMEM((2, 2, 2, nodes, species, cy, cz), f32),
            pltpu.VMEM((species, planes, cy, cz), f32),
            pltpu.VMEM((2, species, 2, cy, cz), f32),
            pltpu.VMEM((n_tm, 2, species, 2, cy, cz), f32),
            pltpu.VMEM((species, planes, cy, cz), f32),
            pltpu.VMEM((n_tm, species, planes, cy, cz), f32),
            dma, dma((species,)),
            dma((2, 2)), dma((2, 2)),
            dma((2, 2, species)), dma((2, 2, species)),
            dma((n_tm, 2)), dma((n_tm, 2)),
            dma((n_tm, species)), dma((n_tm, species)),
        ],
        compiler_params=pltpu.CompilerParams(
            collective_id=0, has_side_effects=True, vmem_limit_bytes=60 * 1024 * 1024
        ),
        cost_estimate=pl.CostEstimate(
            flops=2 * 60 * first_guess.size, bytes_accessed=9 * first_guess.size,
            transcendentals=0),
    )(first_guess, initial_state, diffusivity, coupling, growth_rates)


def solution(mesh):
    in_specs = (
        P(None, ("groups", "space"), None, None),
        P("tm", None, ("groups", "space"), None, None),
        P(None, ("groups", "space"), None, None),
        P(),
        P(),
    )
    out_specs = P("tm", None, ("groups", "space"), None, None)
    return jax.shard_map(
        functools.partial(on_device, mesh.shape["tm"], mesh.shape["space"]),
        mesh=mesh, in_specs=in_specs, out_specs=out_specs, check_vma=False,
    )
```

```python
import functools

import jax
import jax.numpy as jnp
from jax import lax
from jax.experimental import pallas as pl
from jax.experimental.pallas import tpu as pltpu
from jax.sharding import PartitionSpec as P

MESH = pl.DeviceIdType.MESH
slab_span = 0.025


def evaluate(coeffs, point):
    result = 0.0
    for entry in reversed(coeffs):
        result = result * point + entry
    return result


def quadrature(node_count):
    node_pos = [(index + 0.5) / node_count for index in range(node_count)]
    within_rows = [[0.0] * node_count for row_no in range(node_count)]
    whole_row = [0.0] * node_count
    for column in range(node_count):
        coeffs = [1.0]
        scale_value = 1.0
        for other_node in range(node_count):
            if other_node != column:
                shifted = [0.0] + coeffs
                for degree in range(len(coeffs)):
                    shifted[degree] = shifted[degree] - node_pos[other_node] * coeffs[degree]
                coeffs = shifted
                scale_value = scale_value * (node_pos[column] - node_pos[other_node])
        antider = [0.0] + [
            coeffs[degree] / (degree + 1) / scale_value for degree in range(len(coeffs))
        ]
        for row_no in range(node_count):
            within_rows[row_no][column] = evaluate(antider, node_pos[row_no]) * slab_span
        whole_row[column] = evaluate(antider, 1.0) * slab_span
    return (within_rows, whole_row)


def kernel(
    n_tm, n_z, within, whole,
    guess, init_in, diff_in, coupling_in, growth_in, out,
    init, diff, coupling, growth, small_sem,
    u, base, u1, hal, d12, tsend1, trecv1, tsend2, trecv2,
    load_sem, out_sem, hs1, hr1, hs2, hr2, ts1, tr1, ts2, tr2,
):
    nodes, species, planes = u.shape[:3]
    tm = lax.axis_index("tm")
    z = lax.axis_index("space")
    groups = ((1, 2), (0, planes - 1))

    can_send = (z < n_z - 1, z > 0)
    has_recv = (z > 0, z < n_z - 1)

    def target(side):
        return {"space": z + 1} if side == 0 else {"space": z - 1}

    def edge(side, dist):
        return planes - 1 - dist if side == 0 else dist

    def halo1(side, dist):
        return pltpu.make_async_remote_copy(
            src_ref=guess.at[:, :, edge(side, dist)],
            dst_ref=hal.at[0, side, dist],
            send_sem=hs1.at[side, dist], recv_sem=hr1.at[side, dist],
            device_id=target(side), device_id_type=MESH,
        )

    def halo2(side, dist, s):
        return pltpu.make_async_remote_copy(
            src_ref=u1.at[:, s, edge(side, dist)],
            dst_ref=hal.at[1, side, dist, :, s],
            send_sem=hs2.at[side, dist, s], recv_sem=hr2.at[side, dist, s],
            device_id=target(side), device_id_type=MESH,
        )

    def total1(source, peer, g):
        return pltpu.make_async_remote_copy(
            src_ref=tsend1.at[g], dst_ref=trecv1.at[source, g],
            send_sem=ts1.at[peer, g], recv_sem=tr1.at[source, g],
            device_id={"tm": peer}, device_id_type=MESH,
        )

    def total2(source, peer, s):
        return pltpu.make_async_remote_copy(
            src_ref=tsend2.at[s], dst_ref=trecv2.at[source, s],
            send_sem=ts2.at[peer, s], recv_sem=tr2.at[source, s],
            device_id={"tm": peer}, device_id_type=MESH,
        )

    def loop(count, body, first=0):
        def step(i, carry):
            body(i)
            return carry
        lax.fori_loop(first, count, step, 0)

    load = pltpu.make_async_copy(guess, u, load_sem)
    load.start()
    small = [
        pltpu.make_async_copy(source, target_ref, small_sem.at[i])
        for i, (source, target_ref) in enumerate(
            ((init_in, init), (diff_in, diff), (coupling_in, coupling), (growth_in, growth)))
    ]
    for copy in small:
        copy.start()

    barrier = pltpu.get_barrier_semaphore()
    for side in (0, 1):
        @pl.when(can_send[side])
        def _():
            pl.semaphore_signal(barrier, inc=1, device_id=target(side), device_id_type=MESH)
    for peer in range(n_tm):
        @pl.when(peer != tm)
        def _():
            pl.semaphore_signal(barrier, inc=1, device_id={"tm": peer}, device_id_type=MESH)
    neighbours = (z > 0).astype(jnp.int32) + (z < n_z - 1).astype(jnp.int32)
    pl.semaphore_wait(barrier, neighbours + n_tm - 1)

    for side in (0, 1):
        @pl.when(can_send[side])
        def _():
            halo1(side, 0).start()

    for side in (0, 1):
        @pl.when(jnp.logical_not(has_recv[side]))
        def _():
            def clear(s):
                for k in (0, 1):
                    for dist in (0, 1):
                        hal[k, side, dist, :, s] = jnp.zeros(
                            (nodes,) + hal.shape[5:], jnp.float32)
            loop(species, clear)

    for copy in small:
        copy.wait()
    d12[...] = diff[...] * (1.0 / 12.0)
    load.wait()

    def near_part(ref, s, p):
        c = ref[:, s, p]
        acc = growth[s] * c - c * c * c * (1.0 / 3.0)
        for r in range(species):
            acc = acc + coupling[s, r] * ref[:, r, p]
        near = pltpu.roll(c, 1, 1) + pltpu.roll(c, c.shape[1] - 1, 1)
        near = near + (pltpu.roll(c, 1, 2) + pltpu.roll(c, c.shape[2] - 1, 2))
        far = pltpu.roll(c, 2, 1) + pltpu.roll(c, c.shape[1] - 2, 1)
        far = far + (pltpu.roll(c, 2, 2) + pltpu.roll(c, c.shape[2] - 2, 2))
        for q in (p - 1, p + 1):
            if 0 <= q < planes:
                near = near + ref[:, s, q]
        for q in (p - 2, p + 2):
            if 0 <= q < planes:
                far = far + ref[:, s, q]
        base[:, s, p] = acc + d12[s, p][None] * (16.0 * near - far - 90.0 * c)

    def with_halo(k, s, p):
        if p == 0:
            add = 16.0 * hal[k, 0, 0, :, s] - hal[k, 0, 1, :, s]
        elif p == 1:
            add = -hal[k, 0, 0, :, s]
        elif p == planes - 1:
            add = 16.0 * hal[k, 1, 0, :, s] - hal[k, 1, 1, :, s]
        else:
            add = -hal[k, 1, 0, :, s]
        return base[:, s, p] + d12[s, p][None] * add

    def integrate(f, s, p):
        for m in range(nodes):
            row = within[m][0] * f[0]
            for j in range(1, nodes):
                row = row + within[m][j] * f[j]
            base[m, s, p] = row
        total = whole[0] * f[0]
        for j in range(1, nodes):
            total = total + whole[j] * f[j]
        return total

    def all_near(ref):
        def body(s):
            for p in range(planes):
                near_part(ref, s, p)
        loop(species, body)

    all_near(u)
    for side in (0, 1):
        @pl.when(can_send[side])
        def _():
            halo1(side, 0).wait_send()
            halo1(side, 1).start()
    for g in (0, 1):
        for side in (0, 1):
            @pl.when(has_recv[side])
            def _():
                halo1(side, g).wait_recv()

        def finish(s):
            for i, p in enumerate(groups[g]):
                tsend1[g, s, i] = integrate(with_halo(0, s, p), s, p)
        loop(species, finish)
        loop(n_tm, lambda peer: total1(tm, peer, g).start(), tm + 1)
        loop(tm, lambda source: total1(source, tm, g).wait_recv())

        def advance(s):
            for i, p in enumerate(groups[g]):
                first = lax.fori_loop(
                    0, tm, lambda q, acc: acc + trecv1[q, g, s, i],
                    jnp.zeros(init.shape[2:], jnp.float32))
                u1[:, s, p] = base[:, s, p] + (init[s, p] + first)[None]
            for side in (0, 1):
                @pl.when(can_send[side])
                def _():
                    halo2(side, 1 - g, s).start()
        loop(species, advance)

    all_near(u1)
    for side in (0, 1):
        @pl.when(has_recv[side])
        def _():
            loop(species, lambda s: halo2(side, 1, s).wait_recv())

    def finish2(s):
        for side in (0, 1):
            @pl.when(has_recv[side])
            def _():
                halo2(side, 0, s).wait_recv()
        for p in range(planes):
            tsend2[s, p] = integrate(with_halo(1, s, p), s, p)
        loop(n_tm, lambda peer: total2(tm, peer, s).start(), tm + 1)
    loop(species, finish2)

    def store(s):
        return pltpu.make_async_copy(u.at[:, s], out.at[:, s], out_sem.at[s])

    def last(s):
        def gather(q, acc):
            total2(q, tm, s).wait_recv()
            return acc + trecv2[q, s]
        first = lax.fori_loop(0, tm, gather, init[s])
        u[:, s] = base[:, s] + first[None]
        store(s).start()
    loop(species, last)

    for side in (0, 1):
        @pl.when(can_send[side])
        def _():
            halo1(side, 1).wait_send()
            for dist in (0, 1):
                loop(species, lambda s: halo2(side, dist, s).wait_send())

    def sent(peer):
        for g in (0, 1):
            total1(tm, peer, g).wait_send()
        loop(species, lambda s: total2(tm, peer, s).wait_send())
    loop(n_tm, sent, tm + 1)
    loop(species, lambda s: store(s).wait())


def on_device(n_tm, n_z, initial_state, first_guess, diffusivity, growth_rates, coupling):
    nodes, species, planes, cy, cz = first_guess.shape
    within, whole = quadrature(nodes)
    hbm = pl.BlockSpec(memory_space=pltpu.HBM)
    f32 = jnp.float32
    block = pltpu.VMEM(first_guess.shape, f32)
    dma = pltpu.SemaphoreType.DMA
    return pl.pallas_call(
        functools.partial(kernel, n_tm, n_z, within, whole),
        out_shape=jax.ShapeDtypeStruct(first_guess.shape, f32),
        in_specs=[hbm] * 5,
        out_specs=pl.BlockSpec(memory_space=pl.ANY),
        scratch_shapes=[
            pltpu.VMEM((species, planes, cy, cz), f32),
            pltpu.VMEM((species, planes, cy, cz), f32),
            pltpu.SMEM(coupling.shape, f32),
            pltpu.SMEM(growth_rates.shape, f32),
            dma((4,)),
            block, block, block,
            pltpu.VMEM((2, 2, 2, nodes, species, cy, cz), f32),
            pltpu.VMEM((species, planes, cy, cz), f32),
            pltpu.VMEM((2, species, 2, cy, cz), f32),
            pltpu.VMEM((n_tm, 2, species, 2, cy, cz), f32),
            pltpu.VMEM((species, planes, cy, cz), f32),
            pltpu.VMEM((n_tm, species, planes, cy, cz), f32),
            dma, dma((species,)),
            dma((2, 2)), dma((2, 2)),
            dma((2, 2, species)), dma((2, 2, species)),
            dma((n_tm, 2)), dma((n_tm, 2)),
            dma((n_tm, species)), dma((n_tm, species)),
        ],
        compiler_params=pltpu.CompilerParams(
            collective_id=0, has_side_effects=True, vmem_limit_bytes=32 * 1024 * 1024
        ),
        cost_estimate=pl.CostEstimate(
            flops=2 * 60 * first_guess.size, bytes_accessed=9 * first_guess.size,
            transcendentals=0),
    )(first_guess, initial_state, diffusivity, coupling, growth_rates)


def solution(mesh):
    in_specs = (
        P(None, ("groups", "space"), None, None),
        P("tm", None, ("groups", "space"), None, None),
        P(None, ("groups", "space"), None, None),
        P(),
        P(),
    )
    out_specs = P("tm", None, ("groups", "space"), None, None)
    return jax.shard_map(
        functools.partial(on_device, mesh.shape["tm"], mesh.shape["space"]),
        mesh=mesh, in_specs=in_specs, out_specs=out_specs, check_vma=False,
    )
```

```python
import functools

import jax
import jax.numpy as jnp
from jax import lax
from jax.experimental import pallas as pl
from jax.experimental.pallas import tpu as pltpu
from jax.sharding import PartitionSpec as P

MESH = pl.DeviceIdType.MESH
slab_span = 0.025


def evaluate(coeffs, point):
    result = 0.0
    for entry in reversed(coeffs):
        result = result * point + entry
    return result


def quadrature(node_count):
    node_pos = [(index + 0.5) / node_count for index in range(node_count)]
    within_rows = [[0.0] * node_count for row_no in range(node_count)]
    whole_row = [0.0] * node_count
    for column in range(node_count):
        coeffs = [1.0]
        scale_value = 1.0
        for other_node in range(node_count):
            if other_node != column:
                shifted = [0.0] + coeffs
                for degree in range(len(coeffs)):
                    shifted[degree] = shifted[degree] - node_pos[other_node] * coeffs[degree]
                coeffs = shifted
                scale_value = scale_value * (node_pos[column] - node_pos[other_node])
        antider = [0.0] + [
            coeffs[degree] / (degree + 1) / scale_value for degree in range(len(coeffs))
        ]
        for row_no in range(node_count):
            within_rows[row_no][column] = evaluate(antider, node_pos[row_no]) * slab_span
        whole_row[column] = evaluate(antider, 1.0) * slab_span
    return (within_rows, whole_row)


def kernel(
    n_tm, n_z, within, whole,
    guess, init_in, diff_in, coupling_in, growth_in, out,
    init, diff, coupling, growth, small_sem,
    u, base, u1, hal, d12, tsend1, trecv1, tsend2, trecv2,
    load_sem, out_sem, hs1, hr1, hs2, hr2, ts1, tr1, ts2, tr2,
):
    nodes, species, planes = u.shape[:3]
    tm = lax.axis_index("tm")
    z = lax.axis_index("space")
    groups = ((1, 2), (0, planes - 1))

    can_send = (z < n_z - 1, z > 0)
    has_recv = (z > 0, z < n_z - 1)

    def target(side):
        return {"space": z + 1} if side == 0 else {"space": z - 1}

    def edge(side, dist):
        return planes - 1 - dist if side == 0 else dist

    def halo1(side, dist):
        return pltpu.make_async_remote_copy(
            src_ref=guess.at[:, :, edge(side, dist)],
            dst_ref=hal.at[0, side, dist],
            send_sem=hs1.at[side, dist], recv_sem=hr1.at[side, dist],
            device_id=target(side), device_id_type=MESH,
        )

    def halo2(side, dist, s):
        return pltpu.make_async_remote_copy(
            src_ref=u1.at[:, s, edge(side, dist)],
            dst_ref=hal.at[1, side, dist, :, s],
            send_sem=hs2.at[side, dist, s], recv_sem=hr2.at[side, dist, s],
            device_id=target(side), device_id_type=MESH,
        )

    def total1(source, peer, g):
        return pltpu.make_async_remote_copy(
            src_ref=tsend1.at[g], dst_ref=trecv1.at[source, g],
            send_sem=ts1.at[peer, g], recv_sem=tr1.at[source, g],
            device_id={"tm": peer}, device_id_type=MESH,
        )

    def total2(source, peer, s):
        return pltpu.make_async_remote_copy(
            src_ref=tsend2.at[s], dst_ref=trecv2.at[source, s],
            send_sem=ts2.at[peer, s], recv_sem=tr2.at[source, s],
            device_id={"tm": peer}, device_id_type=MESH,
        )

    def loop(count, body, first=0):
        def step(i, carry):
            body(i)
            return carry
        lax.fori_loop(first, count, step, 0)

    load = pltpu.make_async_copy(guess, u, load_sem)
    load.start()
    small = [
        pltpu.make_async_copy(source, target_ref, small_sem.at[i])
        for i, (source, target_ref) in enumerate(
            ((init_in, init), (diff_in, diff), (coupling_in, coupling), (growth_in, growth)))
    ]
    for copy in small:
        copy.start()

    barrier = pltpu.get_barrier_semaphore()
    for side in (0, 1):
        @pl.when(can_send[side])
        def _():
            pl.semaphore_signal(barrier, inc=1, device_id=target(side), device_id_type=MESH)
    for peer in range(n_tm):
        @pl.when(peer != tm)
        def _():
            pl.semaphore_signal(barrier, inc=1, device_id={"tm": peer}, device_id_type=MESH)
    neighbours = (z > 0).astype(jnp.int32) + (z < n_z - 1).astype(jnp.int32)
    pl.semaphore_wait(barrier, neighbours + n_tm - 1)

    for side in (0, 1):
        @pl.when(can_send[side])
        def _():
            halo1(side, 0).start()
            halo1(side, 1).start()

    for side in (0, 1):
        @pl.when(jnp.logical_not(has_recv[side]))
        def _():
            def clear(s):
                for k in (0, 1):
                    for dist in (0, 1):
                        hal[k, side, dist, :, s] = jnp.zeros(
                            (nodes,) + hal.shape[5:], jnp.float32)
            loop(species, clear)

    for copy in small:
        copy.wait()
    d12[...] = diff[...] * (1.0 / 12.0)
    load.wait()

    def near_part(ref, s, p):
        c = ref[:, s, p]
        acc = growth[s] * c - c * c * c * (1.0 / 3.0)
        for r in range(species):
            acc = acc + coupling[s, r] * ref[:, r, p]
        near = pltpu.roll(c, 1, 1) + pltpu.roll(c, c.shape[1] - 1, 1)
        near = near + (pltpu.roll(c, 1, 2) + pltpu.roll(c, c.shape[2] - 1, 2))
        far = pltpu.roll(c, 2, 1) + pltpu.roll(c, c.shape[1] - 2, 1)
        far = far + (pltpu.roll(c, 2, 2) + pltpu.roll(c, c.shape[2] - 2, 2))
        for q in (p - 1, p + 1):
            if 0 <= q < planes:
                near = near + ref[:, s, q]
        for q in (p - 2, p + 2):
            if 0 <= q < planes:
                far = far + ref[:, s, q]
        base[:, s, p] = acc + d12[s, p][None] * (16.0 * near - far - 90.0 * c)

    def with_halo(k, s, p):
        if p == 0:
            add = 16.0 * hal[k, 0, 0, :, s] - hal[k, 0, 1, :, s]
        elif p == 1:
            add = -hal[k, 0, 0, :, s]
        elif p == planes - 1:
            add = 16.0 * hal[k, 1, 0, :, s] - hal[k, 1, 1, :, s]
        else:
            add = -hal[k, 1, 0, :, s]
        return base[:, s, p] + d12[s, p][None] * add

    def integrate(f, s, p):
        for m in range(nodes):
            row = within[m][0] * f[0]
            for j in range(1, nodes):
                row = row + within[m][j] * f[j]
            base[m, s, p] = row
        total = whole[0] * f[0]
        for j in range(1, nodes):
            total = total + whole[j] * f[j]
        return total

    def all_near(ref):
        def body(s):
            for p in range(planes):
                near_part(ref, s, p)
        loop(species, body)

    all_near(u)
    for side in (0, 1):
        @pl.when(can_send[side])
        def _():
            halo1(side, 0).wait_send()
    for g in (0, 1):
        for side in (0, 1):
            @pl.when(has_recv[side])
            def _():
                halo1(side, g).wait_recv()

        def finish(s):
            for i, p in enumerate(groups[g]):
                tsend1[g, s, i] = integrate(with_halo(0, s, p), s, p)
        loop(species, finish)
        loop(n_tm, lambda peer: total1(tm, peer, g).start(), tm + 1)
        loop(tm, lambda source: total1(source, tm, g).wait_recv())

        def advance(s):
            for i, p in enumerate(groups[g]):
                first = lax.fori_loop(
                    0, tm, lambda q, acc: acc + trecv1[q, g, s, i],
                    jnp.zeros(init.shape[2:], jnp.float32))
                u1[:, s, p] = base[:, s, p] + (init[s, p] + first)[None]
            for side in (0, 1):
                @pl.when(can_send[side])
                def _():
                    halo2(side, 1 - g, s).start()
        loop(species, advance)

    all_near(u1)
    for side in (0, 1):
        @pl.when(has_recv[side])
        def _():
            loop(species, lambda s: halo2(side, 1, s).wait_recv())

    def finish2(s):
        for side in (0, 1):
            @pl.when(has_recv[side])
            def _():
                halo2(side, 0, s).wait_recv()
        for p in range(planes):
            tsend2[s, p] = integrate(with_halo(1, s, p), s, p)
        loop(n_tm, lambda peer: total2(tm, peer, s).start(), tm + 1)
    loop(species, finish2)

    def store(s):
        return pltpu.make_async_copy(u.at[:, s], out.at[:, s], out_sem.at[s])

    def last(s):
        def gather(q, acc):
            total2(q, tm, s).wait_recv()
            return acc + trecv2[q, s]
        first = lax.fori_loop(0, tm, gather, init[s])
        u[:, s] = base[:, s] + first[None]
        store(s).start()
    loop(species, last)

    for side in (0, 1):
        @pl.when(can_send[side])
        def _():
            halo1(side, 1).wait_send()
            for dist in (0, 1):
                loop(species, lambda s: halo2(side, dist, s).wait_send())

    def sent(peer):
        for g in (0, 1):
            total1(tm, peer, g).wait_send()
        loop(species, lambda s: total2(tm, peer, s).wait_send())
    loop(n_tm, sent, tm + 1)
    loop(species, lambda s: store(s).wait())


def on_device(n_tm, n_z, initial_state, first_guess, diffusivity, growth_rates, coupling):
    nodes, species, planes, cy, cz = first_guess.shape
    within, whole = quadrature(nodes)
    hbm = pl.BlockSpec(memory_space=pltpu.HBM)
    f32 = jnp.float32
    block = pltpu.VMEM(first_guess.shape, f32)
    dma = pltpu.SemaphoreType.DMA
    return pl.pallas_call(
        functools.partial(kernel, n_tm, n_z, within, whole),
        out_shape=jax.ShapeDtypeStruct(first_guess.shape, f32),
        in_specs=[hbm] * 5,
        out_specs=hbm,
        scratch_shapes=[
            pltpu.VMEM((species, planes, cy, cz), f32),
            pltpu.VMEM((species, planes, cy, cz), f32),
            pltpu.SMEM(coupling.shape, f32),
            pltpu.SMEM(growth_rates.shape, f32),
            dma((4,)),
            block, block, block,
            pltpu.VMEM((2, 2, 2, nodes, species, cy, cz), f32),
            pltpu.VMEM((species, planes, cy, cz), f32),
            pltpu.VMEM((2, species, 2, cy, cz), f32),
            pltpu.VMEM((n_tm, 2, species, 2, cy, cz), f32),
            pltpu.VMEM((species, planes, cy, cz), f32),
            pltpu.VMEM((n_tm, species, planes, cy, cz), f32),
            dma, dma((species,)),
            dma((2, 2)), dma((2, 2)),
            dma((2, 2, species)), dma((2, 2, species)),
            dma((n_tm, 2)), dma((n_tm, 2)),
            dma((n_tm, species)), dma((n_tm, species)),
        ],
        compiler_params=pltpu.CompilerParams(
            collective_id=0, has_side_effects=True, vmem_limit_bytes=60 * 1024 * 1024
        ),
        cost_estimate=pl.CostEstimate(
            flops=2 * 60 * first_guess.size, bytes_accessed=9 * first_guess.size,
            transcendentals=0),
    )(first_guess, initial_state, diffusivity, coupling, growth_rates)


def solution(mesh):
    in_specs = (
        P(None, ("groups", "space"), None, None),
        P("tm", None, ("groups", "space"), None, None),
        P(None, ("groups", "space"), None, None),
        P(),
        P(),
    )
    out_specs = P("tm", None, ("groups", "space"), None, None)
    return jax.shard_map(
        functools.partial(on_device, mesh.shape["tm"], mesh.shape["space"]),
        mesh=mesh, in_specs=in_specs, out_specs=out_specs, check_vma=False,
    )
```
